128 devices in a mesh: seq: 16 (over z, y), exp: 8 (over x, core).
Axes of the slice: x: 4, y: 4, z: 4, core: 2. Of those that a mesh axis runs over, the one named last changes fastest.
Arguments:
- queries: bfloat16 [4096, 6144], P('seq', 'exp'), may hold values from -6 to 6
- key_rows: bfloat16 [4096, 6144], P('seq', 'exp'), may hold values from -6 to 6
- value_rows: bfloat16 [4096, 6144], P('seq', 'exp'), may hold values from -6 to 6
- log_decay: float32 [4096, 48], P('seq', 'exp'), may hold values from -1 to 0, as said below
- residual: bfloat16 [4096, 6144], P('seq', 'exp'), may hold values from -6 to 6
- head_gain: float32 [6144], P('exp'), may hold values from 0.1 to 1.9
- moe_gain: float32 [6144], replicated, may hold values from 0.1 to 1.9
- routes: int32 [4096, 2], P(('seq', 'exp')), may hold values from 0 to 7, all different within a row; in each aligned block of 32 rows (0 to 31, 32 to 63, ...) at most 10 rows name the same one
- route_weight: float32 [4096, 2], P(('seq', 'exp')), may hold values from 0.2 to 1
- up_weight: bfloat16 [8, 6144, 9216], P('exp', None, 'seq'), may hold values from -0.078125 to 0.078125
- down_weight: bfloat16 [8, 9216, 6144], P('exp', 'seq'), may hold values from -0.0625 to 0.0625
Outputs:
- layer_out: bfloat16 [4096, 6144], P(('seq', 'exp'))
The draws below stay inside these ranges and needn't reach their ends.
Inputs may be any that keep to these rules, and one draw needn't show every extreme that they name: `log_decay`: every entry is negative. `routes`: A row names two different experts. In each aligned block of 32 rows no expert is named more than 10 times, a bound that some block reaches.
All inputs are finite; a program needn't handle non-finite values.
Results may differ from the reference program's by a relative error of at most 0.012.
Values may be sent and summed in bfloat16 or wider, within the bound.
No kernel may reach another device: no remote copies, remote signals or barrier semaphores. Data moves between devices by JAX's collectives and lax.ppermute only.
A program may use at most 192 MiB of HBM per device.

```python
import math
import jax
import jax.numpy as jnp
import numpy as np
from jax import lax

HEAD_TOTAL = 48
HEAD_DIM = 128
D = 6144
BLK = 256
TOK_DEV = 256
TOKEN_TOTAL = 4096
EXPERTS = 8
EXP_HID = 9216
ROWS_DEV = 32
CAP = 10
N_SEQ = 16


def draw_log_decay(key, part):
    key = jax.random.fold_in(key, 7)
    random_subkeys = jax.random.split(key, 7)
    fast_share = 0.5
    fast_heads = jax.random.bernoulli(random_subkeys[0], fast_share, (HEAD_TOTAL,))
    fast_rate = jnp.exp(jax.random.uniform(random_subkeys[1], (HEAD_TOTAL,), jnp.float32, math.log(1.0 / 50.0), math.log(1.0 / 30.0)))
    slow_rate = jnp.exp(jax.random.uniform(random_subkeys[2], (HEAD_TOTAL,), jnp.float32, math.log(0.05), math.log(0.3))) * (math.log(10.0) / TOKEN_TOTAL)
    baseline_decay_rate = jnp.where(fast_heads, fast_rate, slow_rate)
    per_device_scale = jnp.exp(jax.random.uniform(random_subkeys[3], (TOKEN_TOTAL // TOK_DEV, HEAD_TOTAL), jnp.float32, math.log(0.5), math.log(2.0)))
    per_device_scale = jnp.repeat(per_device_scale, TOK_DEV, axis=0)
    random_noise = jax.random.uniform(random_subkeys[4], (TOKEN_TOTAL, HEAD_TOTAL), jnp.float32, 0.5, 2.0)
    spike_locations = jax.random.randint(random_subkeys[5], (2,), 0, TOKEN_TOTAL)
    spike_mask = jnp.any(jnp.arange(TOKEN_TOTAL)[:, None] == spike_locations[None, :], axis=1).astype(jnp.float32)
    spike_loss = -jnp.log(jax.random.uniform(random_subkeys[6], (TOKEN_TOTAL, HEAD_TOTAL), jnp.float32, 0.6, 0.8))
    return -(baseline_decay_rate[None, :] * per_device_scale * random_noise + spike_mask[:, None] * spike_loss)


def level_of(own_key, dims, cuts, smallest, high):
    factor_of = 1.0
    for position, blocks in cuts:
        steps = jax.random.uniform(jax.random.fold_in(jax.random.fold_in(own_key, 6), position), (blocks,), jnp.float32, smallest / len(cuts), high / len(cuts))
        factor_of = factor_of * jnp.repeat(jnp.exp(steps), dims[position] // blocks).reshape((-1,) + (1,) * (len(dims) - 1 - position))
    return factor_of


def deal_out(stream_key, own, number, rows, count, top, most, lean):
    sequence = jax.random.permutation(stream_key, count)
    crowded, common = load_shares(count, rows * top, most, lean, True), load_shares(count, rows * top, most, lean, False)
    places = jnp.arange(count)

    def named(lengths, turn):
        used = int((lengths > 0).sum())
        fixed = max(1, used // 4)
        moved = fixed + (places - fixed + turn * (used - fixed)) % max(1, count - fixed)
        return jnp.zeros((count,), jnp.int32).at[sequence[jnp.where(places < fixed, places, moved)]].set(jnp.asarray(lengths, jnp.int32))

    lengths = jnp.where(number % 4 == 0, named(crowded, number // 4), named(common, number - number // 4 - 1))
    mixed = jax.random.permutation(jax.random.fold_in(own, 3), count)
    donor, receiver = mixed[0:count // 2 * 2:2], mixed[1:count // 2 * 2:2]
    room = jnp.minimum(lengths[donor] - 1, most - lengths[receiver]) // 2
    room = jnp.where((donor == sequence[0]) | (receiver == sequence[0]) | (lengths[receiver] == 0), 0, jnp.maximum(room, 0))
    moved = jax.random.randint(jax.random.fold_in(own, 4), (count // 2,), 0, 1 << 20) % (room + 1)
    lengths = lengths.at[donor].add(-moved).at[receiver].add(moved)
    members = jnp.searchsorted(jnp.cumsum(lengths), jnp.arange(rows * top), side="right").astype(jnp.int32)
    grid = members.reshape(top, rows).T
    grid = grid[jax.random.permutation(jax.random.fold_in(own, 1), rows)]
    turn = jax.random.randint(jax.random.fold_in(own, 2), (rows, 1), 0, top)
    return jnp.take_along_axis(grid, (jnp.arange(top)[None, :] + turn) % top, axis=1)


def load_shares(number_of, total, limit, skew, full):
    weights = [(1 << 20) // math.isqrt(rank ** skew) + 1 for rank in range(1, number_of + 1)]
    largest = limit if full else min(limit, max(-(-total // number_of), total * weights[0] // sum(weights)))
    least = 1 if total - largest >= number_of - 1 else 0
    counts, rest = [largest] + [least] * (number_of - 1), total - largest - least * (number_of - 1)
    while rest > 0:
        movable = [i for i in range(1, number_of) if counts[i] < largest] or [i for i in range(1, number_of) if counts[i] < limit]
        pool, left = sum([weights[i] for i in movable]), rest
        for i in movable:
            more = min(limit - counts[i], max(1, left * weights[i] // pool), rest)
            counts[i] = counts[i] + more
            rest = rest - more
    return np.array(counts)


def centred(stream_key, shape, deviation, reach, cuts=(), held_as=jnp.bfloat16):
    loudness = level_of(stream_key, shape, cuts, -0.22, 0.18) if cuts else 1.0
    result = jax.random.normal(stream_key, shape, jnp.float32) * deviation * loudness
    return jnp.minimum(jnp.maximum(result, -reach), reach).astype(held_as)


def setup_inputs(seed: int = 0) -> dict:
    key_of = jax.random.split(jax.random.key(seed), 12)
    queries = centred(key_of[0], (TOKEN_TOTAL, D), 1.0, 6.0, ((0, 16), (1, 8)))
    key_rows = centred(key_of[1], (TOKEN_TOTAL, D), 1.0, 6.0, ((0, 16), (1, 8)))
    value_rows = centred(key_of[2], (TOKEN_TOTAL, D), 1.0, 6.0, ((0, 16), (1, 8)))
    log_decay = draw_log_decay(jax.random.fold_in(key_of[11], 71), 0)
    residual = centred(key_of[4], (TOKEN_TOTAL, D), 1.0, 6.0, ((0, 16), (1, 8)))
    head_gain = jnp.clip(1.0 + 0.18 * jax.random.normal(key_of[5], (D,), jnp.float32), 0.1, 1.9)
    moe_gain = jnp.clip(1.0 + 0.18 * jax.random.normal(key_of[6], (D,), jnp.float32), 0.1, 1.9)
    routes_keys = jax.random.split(jax.random.fold_in(key_of[7], 1), TOKEN_TOTAL // ROWS_DEV)
    routes_turns = jax.random.permutation(jax.random.fold_in(key_of[7], 3), TOKEN_TOTAL // ROWS_DEV)
    routes = jax.vmap(lambda own, number: deal_out(jax.random.fold_in(key_of[7], 2), own, number, ROWS_DEV, EXPERTS, 2, CAP, 2))(routes_keys, routes_turns).reshape((TOKEN_TOTAL, 2))
    route_weight = jnp.clip(0.2 + 0.8 * jax.random.uniform(key_of[8], (TOKEN_TOTAL, 2), jnp.float32) ** level_of(key_of[8], (TOKEN_TOTAL, 2), ((0, 128),), -0.2, 0.2), 0.2, 1.0)
    up_weight = centred(key_of[9], (EXPERTS, D, EXP_HID), D ** -0.5, 0.078125, ((0, 8), (2, 16)))
    down_weight = centred(key_of[10], (EXPERTS, EXP_HID, D), EXP_HID ** -0.5, 0.0625, ((0, 8), (1, 16)))
    return {"queries": queries, "key_rows": key_rows, "value_rows": value_rows, "log_decay": log_decay, "residual": residual, "head_gain": head_gain, "moe_gain": moe_gain, "routes": routes, "route_weight": route_weight, "up_weight": up_weight, "down_weight": down_weight}


def rounded(values):
    return lax.optimization_barrier(values.astype(jnp.bfloat16)).astype(jnp.float32)

def block_step(carry_state, blocks_in):
    query_blk, key_blk, value_blk, decay_blk = blocks_in
    cumulative = jnp.cumsum(decay_blk, axis=0)
    block_total = cumulative[-1]
    scores = jnp.einsum('thd,jhd->htj', query_blk.astype(jnp.float32), key_blk.astype(jnp.float32), precision=lax.Precision.HIGHEST)
    levels = jnp.transpose(cumulative)
    spread = levels[:, :, None] - levels[:, None, :]
    causal = jnp.tril(jnp.ones((BLK, BLK), dtype=bool))[None]
    weights = rounded(jnp.where(causal, jnp.exp(jnp.where(causal, spread, 0.0)), 0.0) * scores)
    inner_part = jnp.einsum('htj,jhd->thd', weights, value_blk.astype(jnp.float32), precision=lax.Precision.HIGHEST)
    query_faded = jnp.exp(cumulative)[:, :, None] * query_blk.astype(jnp.float32)
    carried_part = jnp.einsum('thd,hde->the', query_faded, carry_state, precision=lax.Precision.HIGHEST)
    key_faded = rounded(jnp.exp(block_total[None, :] - cumulative)[:, :, None] * key_blk.astype(jnp.float32))
    next_state = jnp.exp(block_total)[:, None, None] * carry_state + jnp.einsum('jhd,jhe->hde', key_faded, value_blk.astype(jnp.float32), precision=lax.Precision.HIGHEST)
    return (next_state, carried_part + inner_part)

def reference(queries, key_rows, value_rows, log_decay, residual, head_gain, moe_gain, routes, route_weight, up_weight, down_weight):
    block_count = TOKEN_TOTAL // BLK
    shaped = (block_count, BLK, HEAD_TOTAL, HEAD_DIM)
    blocks_in = (queries.reshape(shaped), key_rows.reshape(shaped), value_rows.reshape(shaped), log_decay.reshape(block_count, BLK, HEAD_TOTAL))
    start_state = jnp.zeros((HEAD_TOTAL, HEAD_DIM, HEAD_DIM), jnp.float32)
    ignored, attention = lax.scan(block_step, start_state, blocks_in)
    attention = attention.reshape(TOKEN_TOTAL, HEAD_TOTAL, HEAD_DIM)
    mean_square = lax.optimization_barrier(jnp.mean(attention * attention, axis=-1, keepdims=True))
    normed = attention * lax.rsqrt(mean_square + 1e-06) * head_gain.reshape(HEAD_TOTAL, HEAD_DIM)
    mixed_rows = (residual.astype(jnp.float32) + normed.reshape(TOKEN_TOTAL, D)).astype(jnp.bfloat16)
    mixed_float = mixed_rows.astype(jnp.float32)
    row_square = lax.optimization_barrier(jnp.mean(mixed_float * mixed_float, axis=-1, keepdims=True))
    norm_rows = (mixed_float * lax.rsqrt(row_square + 1e-06) * moe_gain).astype(jnp.bfloat16)
    pieces = N_SEQ
    piece_width = EXP_HID // pieces
    max_rows = TOKEN_TOTAL // ROWS_DEV * CAP
    flat_ids = routes.reshape(-1)
    padded_rows = jnp.concatenate([norm_rows, jnp.zeros((1, D), jnp.bfloat16)], axis=0)
    padded_weight = jnp.concatenate([route_weight.reshape(-1), jnp.zeros((1,), jnp.float32)], axis=0)

    def per_expert(accumulated, expert):
        pair_index = jnp.nonzero(flat_ids == expert, size=max_rows, fill_value=2 * TOKEN_TOTAL)[0].astype(jnp.int32)
        token_index = pair_index // 2
        picked = padded_rows[token_index]
        up_piece = up_weight[expert]
        down_piece = down_weight[expert]
        activated = jax.nn.silu(jnp.dot(picked, up_piece, preferred_element_type=jnp.float32)).astype(jnp.bfloat16)
        expert_out = jnp.zeros((max_rows, D), jnp.float32)
        for piece in range(pieces):
            lo_col = piece * piece_width
            term = jnp.dot(activated[:, lo_col:lo_col + piece_width], down_piece[lo_col:lo_col + piece_width], preferred_element_type=jnp.float32)
            expert_out = expert_out + rounded(term)
        contribution = expert_out * padded_weight[pair_index][:, None]
        accumulated = accumulated.at[token_index].add(contribution, mode='drop')
        return (accumulated, None)
    accumulated, ignored_too = lax.scan(per_expert, jnp.zeros((TOKEN_TOTAL, D), jnp.float32), jnp.arange(EXPERTS, dtype=jnp.int32))
    return (mixed_float + accumulated).astype(jnp.bfloat16)
```

```python
import jax
import jax.numpy as jnp
from jax import lax
from jax.experimental import pallas as pl
from jax.experimental.pallas import tpu as pltpu
from jax.sharding import Mesh
from jax.sharding import PartitionSpec as P

HEAD_DIM = 128
BLK = 256
EXPERTS = 8
CAP = 10
ROWS = 32
LOG_ROWS = 16
VMEM = 56 * 1024 * 1024
F32 = jnp.float32
BF16 = jnp.bfloat16
HIGH = lax.Precision.HIGHEST
SEQ = ("z", "y")
EXP = ("x", "core")


def params():
    return pltpu.CompilerParams(vmem_limit_bytes=VMEM)


def whole():
    return pl.BlockSpec(memory_space=pltpu.VMEM)


def call(kernel, out, *args):
    many = isinstance(out, (list, tuple))
    return pl.pallas_call(
        kernel,
        out_shape=out,
        in_specs=[whole()] * len(args),
        out_specs=[whole()] * len(out) if many else whole(),
        compiler_params=params(),
    )(*args)


def shape(dims, dtype):
    return jax.ShapeDtypeStruct(dims, dtype)


def split3(value):
    first = value.astype(BF16)
    rest = value - first.astype(F32)
    second = rest.astype(BF16)
    third = (rest - second.astype(F32)).astype(BF16)
    return first, second, third


def cumulated(decay):
    row = lax.broadcasted_iota(jnp.int32, (BLK, BLK), 0)
    col = lax.broadcasted_iota(jnp.int32, (BLK, BLK), 1)
    lower = (col <= row).astype(F32)
    return jnp.dot(lower, decay, preferred_element_type=F32, precision=HIGH)


def log_lines(logs):
    heads = logs.shape[1]
    wide = jnp.concatenate([logs, jnp.zeros((1, HEAD_DIM - heads), F32)], axis=1)
    parts = [p.astype(F32) for p in split3(wide)]
    lines = jnp.concatenate(parts + [jnp.zeros((LOG_ROWS - 3, HEAD_DIM), F32)], axis=0)
    return lines.astype(BF16)


def state_kernel(key_ref, value_ref, decay_ref, out_ref):
    heads = decay_ref.shape[1]
    cumul = cumulated(decay_ref[...])
    total = cumul[BLK - 1 :, :]
    fading = jnp.exp(total - cumul)
    for h in range(heads):
        cols = slice(h * HEAD_DIM, (h + 1) * HEAD_DIM)
        faded = (fading[:, h : h + 1] * key_ref[:, cols].astype(F32)).astype(BF16)
        own = lax.dot_general(
            faded, value_ref[:, cols], (((0,), (0,)), ((), ())), preferred_element_type=F32
        )
        out_ref[cols, :] = own.astype(BF16)
    out_ref[heads * HEAD_DIM :, :] = log_lines(total)


def inner_kernel(query_ref, key_ref, value_ref, decay_ref, out_ref):
    heads = decay_ref.shape[1]
    decay = decay_ref[...]
    cumul = cumulated(decay)
    row = lax.broadcasted_iota(jnp.int32, (BLK, BLK), 0)
    col = lax.broadcasted_iota(jnp.int32, (BLK, BLK), 1)
    upper = (row <= col).astype(F32)
    across = lax.dot_general(
        decay, upper, (((0,), (0,)), ((), ())), preferred_element_type=F32, precision=HIGH
    )
    causal = col <= row
    for h in range(heads):
        cols = slice(h * HEAD_DIM, (h + 1) * HEAD_DIM)
        scores = lax.dot_general(
            query_ref[:, cols],
            key_ref[:, cols],
            (((1,), (1,)), ((), ())),
            preferred_element_type=F32,
        )
        spread = cumul[:, h : h + 1] - across[h : h + 1, :]
        weights = jnp.where(causal, jnp.exp(jnp.where(causal, spread, 0.0)) * scores, 0.0)
        out_ref[:, cols] = jnp.dot(
            weights.astype(BF16), value_ref[:, cols], preferred_element_type=F32
        )


def read_logs(ref, i, heads):
    rows = ref[i, heads * HEAD_DIM :, :].astype(F32)
    return rows[0:1] + rows[1:2] + rows[2:3]


def line_kernel(place_ref, gathered_ref, line_ref, before_ref, log_ref):
    heads = gathered_ref.shape[1] // HEAD_DIM
    mine = place_ref[1]
    count = gathered_ref.shape[0]
    logs = [read_logs(gathered_ref, i, heads) for i in range(count)]
    below = [jnp.where(i < mine, logs[i], 0.0) for i in range(count)]
    to_end, to_me = [], []
    for i in range(count):
        to_end.append(jnp.exp(sum(logs[i + 1 :], jnp.zeros_like(logs[0]))))
        to_me.append(
            jnp.where(i < mine, jnp.exp(sum(below[i + 1 :], jnp.zeros_like(logs[0]))), 0.0)
        )
    for h in range(heads):
        rows = slice(h * HEAD_DIM, (h + 1) * HEAD_DIM)
        end = jnp.zeros((HEAD_DIM, HEAD_DIM), F32)
        me = jnp.zeros((HEAD_DIM, HEAD_DIM), F32)
        for i in range(count):
            state = gathered_ref[i, rows, :].astype(F32)
            end = end + to_end[i][:, h : h + 1] * state
            me = me + to_me[i][:, h : h + 1] * state
        line_ref[rows, :] = end.astype(BF16)
        before_ref[rows, :] = me
    line_ref[heads * HEAD_DIM :, :] = log_lines(sum(logs)[:, :heads])
    log_ref[...] = jnp.broadcast_to(sum(below), log_ref.shape)


def mix_kernel(
    place_ref,
    query_ref,
    decay_ref,
    inner_ref,
    residual_ref,
    gain_ref,
    lines_ref,
    before_ref,
    log_ref,
    routes_ref,
    mixed_ref,
    packed_ref,
):
    heads = decay_ref.shape[1]
    mine = place_ref[0]
    count = lines_ref.shape[0]
    logs = [read_logs(lines_ref, i, heads) for i in range(count)]
    below = [jnp.where(i < mine, logs[i], 0.0) for i in range(count)]
    here = log_ref[0:1, :]
    factors = [
        jnp.where(i < mine, jnp.exp(sum(below[i + 1 :], here)), 0.0) for i in range(count)
    ]
    fade = jnp.exp(cumulated(decay_ref[...]))
    for h in range(heads):
        cols = slice(h * HEAD_DIM, (h + 1) * HEAD_DIM)
        state = before_ref[cols, :]
        for i in range(count):
            state = state + factors[i][:, h : h + 1] * lines_ref[i, cols, :].astype(F32)
        faded = fade[:, h : h + 1] * query_ref[:, cols].astype(F32)
        attention = inner_ref[:, cols] + jnp.dot(
            faded, state, preferred_element_type=F32, precision=HIGH
        )
        square = jnp.mean(attention * attention, axis=-1, keepdims=True)
        normed = attention * lax.rsqrt(square + 1e-06) * gain_ref[:, cols]
        mixed_ref[:, cols] = (residual_ref[:, cols].astype(F32) + normed).astype(BF16)
    token = lax.broadcasted_iota(jnp.int32, (EXPERTS, BLK), 1)
    expert = lax.broadcasted_iota(jnp.int32, (EXPERTS, BLK), 0)
    names = (expert == routes_ref[0:1, :]) | (expert == routes_ref[1:2, :])
    row = lax.broadcasted_iota(jnp.int32, (BLK, BLK), 0)
    col = lax.broadcasted_iota(jnp.int32, (BLK, BLK), 1)
    earlier = ((row < col) & (row // ROWS == col // ROWS)).astype(BF16)
    rank = jnp.dot(names.astype(BF16), earlier, preferred_element_type=F32).astype(jnp.int32)
    slot = jnp.where(names, token // ROWS * CAP + rank, -1)
    slots = packed_ref.shape[1]
    which = lax.broadcasted_iota(jnp.int32, (slots, BLK), 0)
    mixed = mixed_ref[...]
    for e in range(EXPERTS):
        placer = (which == slot[e : e + 1, :]).astype(BF16)
        packed_ref[e] = jnp.dot(placer, mixed, preferred_element_type=F32).astype(BF16)


def norm_kernel(parts_ref, gain_ref, out_ref):
    parts, _, width = parts_ref.shape
    square = 0.0
    for j in range(parts):
        value = parts_ref[j].astype(F32)
        square = square + jnp.sum(value * value, axis=-1, keepdims=True)
    scale = lax.rsqrt(square / (parts * width) + 1e-06)
    for j in range(parts):
        cols = slice(j * width, (j + 1) * width)
        out_ref[:, cols] = (parts_ref[j].astype(F32) * scale * gain_ref[:, cols]).astype(BF16)


def expert_kernel(rows_ref, up_ref, down_ref, out_ref):
    value = jnp.dot(rows_ref[...], up_ref[...], preferred_element_type=F32)
    hidden = (value / (1.0 + jnp.exp(-value))).astype(BF16)
    out_ref[...] = jnp.dot(hidden, down_ref[...], preferred_element_type=F32).astype(BF16)


def expert_part(rows, up_weight, down_weight, tile):
    total, width = rows.shape
    units = up_weight.shape[-1]
    once = pl.Buffered(1)
    return pl.pallas_call(
        expert_kernel,
        grid=(total // tile,),
        out_shape=shape((total, width), BF16),
        in_specs=[
            pl.BlockSpec((tile, width), lambda i: (i, 0)),
            pl.BlockSpec((None, width, units), lambda i: (0, 0, 0), pipeline_mode=once),
            pl.BlockSpec((None, units, width), lambda i: (0, 0, 0), pipeline_mode=once),
        ],
        out_specs=pl.BlockSpec((tile, width), lambda i: (i, 0)),
        compiler_params=params(),
        cost_estimate=pl.CostEstimate(
            flops=4 * total * width * units,
            bytes_accessed=4 * (total + units) * width,
            transcendentals=total * units,
        ),
    )(rows, up_weight, down_weight)


def combine_kernel(routes_ref, weight_ref, returned_ref, mixed_ref, out_ref):
    rows = out_ref.shape[0]
    routes = routes_ref[...]
    expert = lax.broadcasted_iota(jnp.int32, (rows, EXPERTS), 1)
    names = [expert == routes[:, i : i + 1] for i in range(2)]
    row = lax.broadcasted_iota(jnp.int32, (rows, rows), 0)
    col = lax.broadcasted_iota(jnp.int32, (rows, rows), 1)
    earlier = (col < row).astype(BF16)
    rank = jnp.dot(
        earlier, (names[0] | names[1]).astype(BF16), preferred_element_type=F32
    ).astype(jnp.int32)
    place = lax.broadcasted_iota(jnp.int32, (rows, EXPERTS * CAP), 1)
    blend = jnp.zeros((rows, EXPERTS * CAP), F32)
    for i in range(2):
        slot = jnp.sum(jnp.where(names[i], expert * CAP + rank, 0), axis=1, keepdims=True)
        blend = blend + jnp.where(place == slot, weight_ref[:, i : i + 1], 0.0)
    parts = split3(blend)
    width = mixed_ref.shape[2]
    for j in range(mixed_ref.shape[0]):
        cols = slice(j * width, (j + 1) * width)
        value = returned_ref[:, cols]
        added = sum(jnp.dot(p, value, preferred_element_type=F32) for p in parts)
        out_ref[:, cols] = (mixed_ref[j].astype(F32) + added).astype(BF16)


def per_device(
    queries,
    key_rows,
    value_rows,
    log_decay,
    residual,
    head_gain,
    moe_gain,
    routes,
    route_weight,
    up_weight,
    down_weight,
):
    token_count, width = queries.shape
    heads = log_decay.shape[1]
    model = moe_gain.shape[0]
    exp_count = model // width
    slots = token_count // ROWS * CAP
    place = jnp.stack([lax.axis_index("z"), lax.axis_index("y")]).astype(jnp.int32)
    all_routes = lax.all_gather(routes, EXP, axis=0, tiled=True).T

    state_rows = heads * HEAD_DIM + LOG_ROWS
    sent = call(state_kernel, shape((state_rows, HEAD_DIM), BF16), key_rows, value_rows, log_decay)
    in_line = lax.all_gather(sent, "y", axis=0, tiled=False)
    inner = call(
        inner_kernel, shape((token_count, width), F32), queries, key_rows, value_rows, log_decay
    )
    scalar = pl.BlockSpec(memory_space=pltpu.SMEM)
    line, before, line_log = pl.pallas_call(
        line_kernel,
        out_shape=[
            shape((state_rows, HEAD_DIM), BF16),
            shape((heads * HEAD_DIM, HEAD_DIM), F32),
            shape((8, HEAD_DIM), F32),
        ],
        in_specs=[scalar, whole()],
        out_specs=[whole()] * 3,
        compiler_params=params(),
    )(place, in_line)
    lines = lax.all_gather(line, "z", axis=0, tiled=False)
    mixed, packed = pl.pallas_call(
        mix_kernel,
        out_shape=[
            shape((token_count, width), BF16),
            shape((EXPERTS, slots, width), BF16),
        ],
        in_specs=[scalar] + [whole()] * 9,
        out_specs=[whole()] * 2,
        compiler_params=params(),
    )(
        place,
        queries,
        log_decay,
        inner,
        residual,
        head_gain.reshape(1, width),
        lines,
        before,
        line_log,
        all_routes,
    )
    parts = lax.all_to_all(packed, EXP, split_axis=0, concat_axis=0, tiled=True)
    home = lax.all_to_all(
        mixed.reshape(exp_count, ROWS, width), EXP, split_axis=0, concat_axis=0, tiled=True
    )
    normed = call(norm_kernel, shape((slots, model), BF16), parts, moe_gain.reshape(1, model))
    rows = lax.all_gather(normed, SEQ, axis=0, tiled=True)
    partial = expert_part(rows, up_weight, down_weight, 256)
    summed = lax.psum_scatter(partial, SEQ, scatter_dimension=0, tiled=True)
    back = lax.all_to_all(
        summed.reshape(exp_count, CAP * model // HEAD_DIM, HEAD_DIM),
        EXP,
        split_axis=0,
        concat_axis=0,
        tiled=True,
    )
    returned = back.reshape(EXPERTS * CAP, model)
    return call(
        combine_kernel, shape((ROWS, model), BF16), routes, route_weight, returned, home
    )


def solution(mesh):
    fine = Mesh(mesh.devices.reshape(4, 4, 4, 2), ("z", "y", "x", "core"))
    both = ("z", "y", "x", "core")
    return jax.shard_map(
        per_device,
        mesh=fine,
        in_specs=(
            P(SEQ, EXP),
            P(SEQ, EXP),
            P(SEQ, EXP),
            P(SEQ, EXP),
            P(SEQ, EXP),
            P(EXP),
            P(),
            P(both, None),
            P(both, None),
            P(EXP, None, SEQ),
            P(EXP, SEQ, None),
        ),
        out_specs=P(both, None),
        check_vma=False,
    )
```

```python
import jax
import jax.numpy as jnp
from jax import lax
from jax.experimental import pallas as pl
from jax.experimental.pallas import tpu as pltpu
from jax.sharding import Mesh
from jax.sharding import PartitionSpec as P

HEAD_DIM = 128
BLK = 256
EXPERTS = 8
CAP = 10
FIRST = 8
LAST = CAP - FIRST
SIDE = 4
TILE = 256
ROWS = 32
LOG_ROWS = 16
VMEM = 56 * 1024 * 1024
F32 = jnp.float32
BF16 = jnp.bfloat16
HIGH = lax.Precision.HIGHEST
SEQ = ("z", "y")
EXP = ("x", "core")


def params():
    return pltpu.CompilerParams(vmem_limit_bytes=VMEM)


def whole():
    return pl.BlockSpec(memory_space=pltpu.VMEM)


def call(kernel, out, *args):
    many = isinstance(out, (list, tuple))
    return pl.pallas_call(
        kernel,
        out_shape=out,
        in_specs=[whole()] * len(args),
        out_specs=[whole()] * len(out) if many else whole(),
        compiler_params=params(),
    )(*args)


def shape(dims, dtype):
    return jax.ShapeDtypeStruct(dims, dtype)


def split3(value):
    first = value.astype(BF16)
    rest = value - first.astype(F32)
    second = rest.astype(BF16)
    third = (rest - second.astype(F32)).astype(BF16)
    return first, second, third


def cumulated(decay):
    row = lax.broadcasted_iota(jnp.int32, (BLK, BLK), 0)
    col = lax.broadcasted_iota(jnp.int32, (BLK, BLK), 1)
    lower = (col <= row).astype(F32)
    return lax.dot_general(
        lower, decay, (((1,), (1,)), ((), ())), preferred_element_type=F32, precision=HIGH
    )


def log_lines(logs):
    heads = logs.shape[1]
    wide = jnp.concatenate([logs, jnp.zeros((1, HEAD_DIM - heads), F32)], axis=1)
    parts = [p.astype(F32) for p in split3(wide)]
    lines = jnp.concatenate(parts + [jnp.zeros((LOG_ROWS - 3, HEAD_DIM), F32)], axis=0)
    return lines.astype(BF16)


def state_kernel(key_ref, value_ref, decay_ref, out_ref):
    heads = decay_ref.shape[0]
    cumul = cumulated(decay_ref[...])
    total = cumul[BLK - 1 :, :]
    fading = jnp.exp(total - cumul)
    for h in range(heads):
        cols = slice(h * HEAD_DIM, (h + 1) * HEAD_DIM)
        faded = (fading[:, h : h + 1] * key_ref[:, cols].astype(F32)).astype(BF16)
        own = lax.dot_general(
            faded, value_ref[:, cols], (((0,), (0,)), ((), ())), preferred_element_type=F32
        )
        out_ref[cols, :] = own.astype(BF16)
    out_ref[heads * HEAD_DIM :, :] = log_lines(total)


def inner_kernel(query_ref, key_ref, value_ref, decay_ref, out_ref):
    heads = decay_ref.shape[0]
    decay = decay_ref[...]
    cumul = cumulated(decay)
    row = lax.broadcasted_iota(jnp.int32, (BLK, BLK), 0)
    col = lax.broadcasted_iota(jnp.int32, (BLK, BLK), 1)
    upper = (row <= col).astype(F32)
    across = jnp.dot(decay, upper, preferred_element_type=F32, precision=HIGH)
    causal = col <= row
    for h in range(heads):
        cols = slice(h * HEAD_DIM, (h + 1) * HEAD_DIM)
        scores = lax.dot_general(
            query_ref[:, cols],
            key_ref[:, cols],
            (((1,), (1,)), ((), ())),
            preferred_element_type=F32,
        )
        spread = cumul[:, h : h + 1] - across[h : h + 1, :]
        weights = jnp.where(causal, jnp.exp(jnp.where(causal, spread, 0.0)) * scores, 0.0)
        out_ref[:, cols] = jnp.dot(
            weights.astype(BF16), value_ref[:, cols], preferred_element_type=F32
        )


def read_logs(ref, heads):
    rows = ref[heads * HEAD_DIM :, :].astype(F32)
    return rows[0:1] + rows[1:2] + rows[2:3]


def line_kernel(place_ref, *refs):
    states, (line_ref, before_ref, log_ref) = refs[:SIDE], refs[SIDE:]
    heads = line_ref.shape[0] // HEAD_DIM
    mine = place_ref[1]
    spots = [lax.rem(mine - d + SIDE, SIDE) for d in range(SIDE)]
    logs = [read_logs(ref, heads) for ref in states]
    to_end, to_me = [], []
    for i in range(SIDE):
        later = [jnp.where(spots[j] > spots[i], logs[j], 0.0) for j in range(SIDE)]
        between = [jnp.where(spots[j] < mine, later[j], 0.0) for j in range(SIDE)]
        to_end.append(jnp.exp(sum(later)))
        to_me.append(jnp.where(spots[i] < mine, jnp.exp(sum(between)), 0.0))
    for h in range(heads):
        rows = slice(h * HEAD_DIM, (h + 1) * HEAD_DIM)
        end = jnp.zeros((HEAD_DIM, HEAD_DIM), F32)
        me = jnp.zeros((HEAD_DIM, HEAD_DIM), F32)
        for i in range(SIDE):
            state = states[i][rows, :].astype(F32)
            end = end + to_end[i][:, h : h + 1] * state
            me = me + to_me[i][:, h : h + 1] * state
        line_ref[rows, :] = end.astype(BF16)
        before_ref[rows, :] = me
    line_ref[heads * HEAD_DIM :, :] = log_lines(sum(logs)[:, :heads])
    before = [jnp.where(spots[i] < mine, logs[i], 0.0) for i in range(SIDE)]
    log_ref[...] = jnp.broadcast_to(sum(before), log_ref.shape)


def mix_kernel(
    query_ref,
    decay_ref,
    inner_ref,
    residual_ref,
    gain_ref,
    line1_ref,
    line2_ref,
    line3_ref,
    before_ref,
    log_ref,
    routes_ref,
    mixed_ref,
    packed_ref,
):
    heads = decay_ref.shape[0]
    lines = (line1_ref, line2_ref, line3_ref)
    logs = [read_logs(ref, heads) for ref in lines]
    here = log_ref[0:1, :]
    factors = [jnp.exp(sum(logs[:i], here)) for i in range(len(lines))]
    fade = jnp.exp(cumulated(decay_ref[...]))
    for h in range(heads):
        cols = slice(h * HEAD_DIM, (h + 1) * HEAD_DIM)
        state = before_ref[cols, :]
        for factor, ref in zip(factors, lines):
            state = state + factor[:, h : h + 1] * ref[cols, :].astype(F32)
        faded = fade[:, h : h + 1] * query_ref[:, cols].astype(F32)
        attention = inner_ref[:, cols] + jnp.dot(
            faded, state, preferred_element_type=F32, precision=HIGH
        )
        square = jnp.mean(attention * attention, axis=-1, keepdims=True)
        normed = attention * lax.rsqrt(square + 1e-06) * gain_ref[:, cols]
        mixed_ref[:, cols] = (residual_ref[:, cols].astype(F32) + normed).astype(BF16)
    token = lax.broadcasted_iota(jnp.int32, (EXPERTS, BLK), 1)
    expert = lax.broadcasted_iota(jnp.int32, (EXPERTS, BLK), 0)
    names = (expert == routes_ref[0:1, :]) | (expert == routes_ref[1:2, :])
    row = lax.broadcasted_iota(jnp.int32, (BLK, BLK), 0)
    col = lax.broadcasted_iota(jnp.int32, (BLK, BLK), 1)
    earlier = ((row < col) & (row // ROWS == col // ROWS)).astype(BF16)
    rank = jnp.dot(names.astype(BF16), earlier, preferred_element_type=F32).astype(jnp.int32)
    mixed = mixed_ref[...]
    block = token // ROWS
    early = rank < FIRST
    low = block * FIRST + rank
    high = BLK // ROWS * FIRST + block * LAST + rank - FIRST
    slot = jnp.where(names, jnp.where(early, low, high), -1)
    which = lax.broadcasted_iota(jnp.int32, (packed_ref.shape[1], BLK), 0)
    for e in range(EXPERTS):
        placer = (which == slot[e : e + 1, :]).astype(BF16)
        packed_ref[e] = jnp.dot(placer, mixed, preferred_element_type=F32).astype(BF16)


def norm_kernel(parts_ref, gain_ref, first_ref, left_ref, right_ref):
    parts, _, width = parts_ref.shape
    early, half = first_ref.shape[0], parts // 2
    square = 0.0
    for j in range(parts):
        value = parts_ref[j].astype(F32)
        square = square + jnp.sum(value * value, axis=-1, keepdims=True)
    scale = lax.rsqrt(square / (parts * width) + 1e-06)
    for j in range(parts):
        cols = slice(j * width, (j + 1) * width)
        value = (parts_ref[j].astype(F32) * scale * gain_ref[:, cols]).astype(BF16)
        first_ref[:, cols] = value[:early]
        side = left_ref if j < half else right_ref
        side[:, j % half * width : (j % half + 1) * width] = value[early:]


def expert_kernel(plan, counts, refs):
    inputs, outputs, parts = counts
    ins, up, down = refs[:inputs], refs[inputs], refs[inputs + 1]
    outs = refs[inputs + 2 : inputs + 2 + outputs]
    up_here, down_here, rows_here, out_here, weight_sem, in_sem, out_sem = refs[-7:]
    tiles, wide = len(plan), up.shape[1] // parts

    def weight_up(k):
        part = pl.ds(k * wide, wide)
        return pltpu.make_async_copy(up.at[0, part], up_here.at[part], weight_sem.at[k])

    def weight_down(k):
        part = pl.ds(k * wide, wide)
        return pltpu.make_async_copy(
            down.at[0, :, part], down_here.at[:, part], weight_sem.at[parts + k]
        )

    def pieces(t, arrays, here, sems, out):
        for i, (array, index, start, count, row, col) in enumerate(plan[t]):
            far = arrays[array].at[index, pl.ds(start, count)]
            near = here.at[t % 2, pl.ds(row, count), pl.ds(col, far.shape[1])]
            pair = (near, far) if out else (far, near)
            yield pltpu.make_async_copy(*pair, sems.at[t % 2, i])

    def read(t):
        return pieces(t, ins, rows_here, in_sem, False)

    def write(t):
        return pieces(t, outs, out_here, out_sem, True)

    for copy in read(0):
        copy.start()
    for k in range(parts):
        weight_up(k).start()

    def at(t, now, action):
        @pl.when(t == now)
        def _():
            action()

    def wait(copies):
        for copy in copies:
            copy.wait()

    def begin(copies):
        for copy in copies:
            copy.start()

    def step(t, carry):
        slot = lax.rem(t, 2)
        for now in range(tiles):
            at(t, now, lambda now=now: wait(read(now)))
        value = 0.0
        for k in range(parts):
            cols = pl.ds(k * wide, wide)
            at(t, 0, lambda k=k: weight_up(k).wait())
            at(t, 0, lambda k=k: weight_down(k).start())
            value = value + jnp.dot(
                rows_here[slot, :, cols], up_here[cols, :], preferred_element_type=F32
            )
        if tiles > 1:
            at(t, 0, lambda: begin(read(1)))
        hidden = (value / (1.0 + jnp.exp(-value))).astype(BF16)
        for now in range(2, tiles):
            at(t, now, lambda now=now: wait(write(now - 2)))
        for k in range(parts):
            cols = pl.ds(k * wide, wide)
            at(t, 0, lambda k=k: weight_down(k).wait())
            out_here[slot, :, cols] = jnp.dot(
                hidden, down_here[:, cols], preferred_element_type=F32
            ).astype(BF16)
        for now in range(tiles):
            at(t, now, lambda now=now: begin(write(now)))
        for now in range(tiles - 2):
            at(t, now, lambda now=now: begin(read(now + 2)))
        return carry

    lax.fori_loop(0, tiles, step, 0)
    for t in range(max(0, tiles - 2), tiles):
        wait(write(t))


def expert_call(plan, arrays, up_weight, down_weight, tile):
    units, width = down_weight.shape[1:]
    total = len(plan) * tile
    parts = 4
    most = max(len(p) for p in plan)
    counts = (len(arrays), len(arrays), parts)
    anywhere = pl.BlockSpec(memory_space=pl.ANY)

    def kernel(*refs):
        expert_kernel(plan, counts, refs)

    return pl.pallas_call(
        kernel,
        out_shape=[shape(a.shape, BF16) for a in arrays],
        in_specs=[anywhere] * (len(arrays) + 2),
        out_specs=[anywhere] * len(arrays),
        scratch_shapes=[
            pltpu.VMEM((width, units), BF16),
            pltpu.VMEM((units, width), BF16),
            pltpu.VMEM((2, tile, width), BF16),
            pltpu.VMEM((2, tile, width), BF16),
            pltpu.SemaphoreType.DMA((2 * parts,)),
            pltpu.SemaphoreType.DMA((2, most)),
            pltpu.SemaphoreType.DMA((2, most)),
        ],
        compiler_params=params(),
        cost_estimate=pl.CostEstimate(
            flops=6 * total * width * units,
            bytes_accessed=4 * (total + units) * width,
            transcendentals=total * units,
        ),
    )(*arrays, up_weight, down_weight)


def rows_kernel(rows_ref, up_ref, down_ref, out_ref):
    value = jnp.dot(rows_ref[...], up_ref[...], preferred_element_type=F32)
    hidden = (value / (1.0 + jnp.exp(-value))).astype(BF16)
    out_ref[...] = jnp.dot(hidden, down_ref[...], preferred_element_type=F32).astype(BF16)


def expert_rows(rows, up_weight, down_weight):
    total, width = rows.shape
    units = up_weight.shape[-1]
    once = pl.Buffered(1)
    return pl.pallas_call(
        rows_kernel,
        grid=(total // TILE,),
        out_shape=shape((total, width), BF16),
        in_specs=[
            pl.BlockSpec((TILE, width), lambda i: (i, 0)),
            pl.BlockSpec((None, width, units), lambda i: (0, 0, 0), pipeline_mode=once),
            pl.BlockSpec((None, units, width), lambda i: (0, 0, 0), pipeline_mode=once),
        ],
        out_specs=pl.BlockSpec((TILE, width), lambda i: (i, 0)),
        compiler_params=params(),
        cost_estimate=pl.CostEstimate(
            flops=4 * total * width * units,
            bytes_accessed=4 * (total + units) * width,
            transcendentals=total * units,
        ),
    )(rows, up_weight, down_weight)


def expert_halves(left, right, up_weight, down_weight):
    arrays = [a for pair in left + right for a in pair]
    _, rows, half = left[0][0].shape
    plan = [[] for _ in range(SIDE * SIDE * rows // TILE)]
    for z in range(SIDE):
        for y in range(SIDE):
            done = 0
            while done < rows:
                t, row = divmod((z * SIDE + y) * rows + done, TILE)
                count = min(rows - done, TILE - row)
                plan[t].append((2 * z + y // 2, y % 2, done, count, row, 0))
                plan[t].append((2 * (SIDE + y) + z // 2, z % 2, done, count, row, half))
                done += count
    out = expert_call(plan, arrays, up_weight, down_weight, TILE)
    pairs = [(out[2 * i], out[2 * i + 1]) for i in range(2 * SIDE)]
    return pairs[:SIDE], pairs[SIDE:]


def shift(value, axis, step, count=SIDE):
    return lax.ppermute(value, axis, [(i, (i + step) % count) for i in range(count)])


def gather_near(value, axis):
    ring = [value] + [shift(value, axis, d) for d in range(1, SIDE)]
    return jnp.stack(ring[:2]), jnp.stack(ring[2:])


def gather_start(low, high, axis):
    low_after, high_before = shift(low, axis, 1), shift(high, axis, -1)
    return low_after, high_before, shift(high, axis, 1), shift(low, axis, -1)


def gather_end(low, high, started, axis):
    low_after, high_before, high_after, low_before = started
    far = (shift(low_after, axis, 1), shift(high_before, axis, -1))
    return [(low, high), (low_after, high_after), far, (low_before, high_before)]


def total_of(*terms):
    return sum(t.astype(F32) for t in terms).astype(BF16)


def scatter_near(low, high, axis):
    return total_of(
        low[0], shift(low[1], axis, -1), shift(high[0], axis, 2), shift(high[1], axis, 1)
    )


def scatter_start(value, axis):
    to_after = shift(value[2][0], axis, 1)
    to_before = shift(value[2][1], axis, -1)
    return to_after, to_before, shift(value[3][1], axis, 1), shift(value[1][0], axis, -1)


def scatter_end(value, started, axis):
    to_after, to_before, high_after, low_before = started
    low_after = shift(total_of(value[3][0], to_after), axis, 1)
    high_before = shift(total_of(value[1][1], to_before), axis, -1)
    return total_of(value[0][0], low_after, low_before), total_of(
        value[0][1], high_after, high_before
    )


def home_rows(summed):
    lines = summed.reshape(EXPERTS, -1, HEAD_DIM)
    back = lax.all_to_all(lines, EXP, split_axis=0, concat_axis=0, tiled=True)
    return back.reshape(summed.shape)


def gather_routes(routes):
    ours = lax.axis_index("core")
    other = shift(routes, "core", 1, 2)
    pair = jnp.where(ours == 0, jnp.stack([routes, other]), jnp.stack([other, routes]))
    ring = jnp.stack([pair] + [shift(pair, "x", d) for d in range(1, SIDE)])
    distance = (lax.axis_index("x") - jnp.arange(SIDE)) % SIDE
    placed = sum(
        jnp.where((distance == d)[:, None, None, None], ring[d][None], 0) for d in range(SIDE)
    )
    return jnp.transpose(placed, (2, 0, 1, 3)).reshape(2, -1)


def combine_kernel(routes_ref, weight_ref, first_ref, last_ref, mixed_ref, out_ref):
    rows = out_ref.shape[0]
    routes = routes_ref[...]
    expert = lax.broadcasted_iota(jnp.int32, (rows, EXPERTS), 1)
    names = [expert == routes[:, i : i + 1] for i in range(2)]
    row = lax.broadcasted_iota(jnp.int32, (rows, rows), 0)
    col = lax.broadcasted_iota(jnp.int32, (rows, rows), 1)
    earlier = (col < row).astype(BF16)
    ranks = jnp.dot(
        earlier, (names[0] | names[1]).astype(BF16), preferred_element_type=F32
    ).astype(jnp.int32)
    chunks = []
    for ref, low, size in ((first_ref, 0, FIRST), (last_ref, FIRST, LAST)):
        place = lax.broadcasted_iota(jnp.int32, (rows, EXPERTS * size), 1)
        blend = jnp.zeros((rows, EXPERTS * size), F32)
        for i in range(2):
            rank = jnp.sum(jnp.where(names[i], ranks, 0), axis=1, keepdims=True)
            slot = routes[:, i : i + 1] * size + rank - low
            taken = (place == slot) & (rank >= low) & (rank < low + size)
            blend = blend + jnp.where(taken, weight_ref[:, i : i + 1], 0.0)
        chunks.append((ref, split3(blend)))
    width = mixed_ref.shape[2]
    for j in range(mixed_ref.shape[0]):
        cols = slice(j * width, (j + 1) * width)
        value = mixed_ref[j].astype(F32)
        for ref, parts in chunks:
            for p in parts:
                value = value + jnp.dot(p, ref[:, cols], preferred_element_type=F32)
        out_ref[:, cols] = value.astype(BF16)


def per_device(
    queries,
    key_rows,
    value_rows,
    log_decay,
    residual,
    head_gain,
    moe_gain,
    routes,
    route_weight,
    up_weight,
    down_weight,
):
    token_count, width = queries.shape
    heads = log_decay.shape[1]
    half = moe_gain.shape[0] // 2
    model = moe_gain.shape[0]
    exp_count = model // width
    blocks = token_count // ROWS
    place = jnp.stack([lax.axis_index("z"), lax.axis_index("y")]).astype(jnp.int32)
    all_routes = gather_routes(routes.T)
    log_decay = log_decay.T

    state_rows = heads * HEAD_DIM + LOG_ROWS
    sent = call(state_kernel, shape((state_rows, HEAD_DIM), BF16), key_rows, value_rows, log_decay)
    in_line = [sent] + [shift(sent, "y", d) for d in range(1, SIDE)]
    inner = call(
        inner_kernel, shape((token_count, width), F32), queries, key_rows, value_rows, log_decay
    )
    in_line, inner, all_routes = lax.optimization_barrier((in_line, inner, all_routes))
    scalar = pl.BlockSpec(memory_space=pltpu.SMEM)
    line, before, line_log = pl.pallas_call(
        line_kernel,
        out_shape=[
            shape((state_rows, HEAD_DIM), BF16),
            shape((heads * HEAD_DIM, HEAD_DIM), F32),
            shape((8, HEAD_DIM), F32),
        ],
        in_specs=[scalar] + [whole()] * SIDE,
        out_specs=[whole()] * 3,
        compiler_params=params(),
    )(place, *in_line)
    lines = [
        lax.ppermute(line, "z", [(i, i + d) for i in range(SIDE - d)]) for d in range(1, SIDE)
    ]
    mixed, packed = pl.pallas_call(
        mix_kernel,
        out_shape=[
            shape((token_count, width), BF16),
            shape((EXPERTS, blocks * CAP, width), BF16),
        ],
        in_specs=[whole()] * 11,
        out_specs=[whole()] * 2,
        compiler_params=params(),
    )(
        queries,
        log_decay,
        inner,
        residual,
        head_gain.reshape(1, width),
        *lines,
        before,
        line_log,
        all_routes,
    )
    parts = lax.all_to_all(packed, EXP, split_axis=0, concat_axis=0, tiled=True)
    normed, left, right = call(
        norm_kernel,
        [shape((blocks * FIRST, model), BF16)] + [shape((blocks * LAST, half), BF16)] * 2,
        parts,
        moe_gain.reshape(1, model),
    )
    rows = lax.all_gather(normed, SEQ, axis=0, tiled=True)
    left, right = gather_near(left, "y"), gather_near(right, "z")
    left = gather_end(*left, gather_start(*left, "z"), "z")
    right = gather_end(*right, gather_start(*right, "y"), "y")
    left, right = expert_halves(left, right, up_weight, down_weight)
    starts = scatter_start(left, "z"), scatter_start(right, "y")
    rows, starts = lax.optimization_barrier((rows, starts))
    left = scatter_end(left, starts[0], "z")
    right = scatter_end(right, starts[1], "y")

    partial = expert_rows(rows, up_weight, down_weight)
    first = lax.psum_scatter(partial, SEQ, scatter_dimension=0, tiled=True)
    mixed, _ = lax.optimization_barrier((mixed, partial))
    home = lax.all_to_all(
        mixed.reshape(exp_count, ROWS, width), EXP, split_axis=0, concat_axis=0, tiled=True
    )
    left, right = scatter_near(*left, "y"), scatter_near(*right, "z")
    last = home_rows(jnp.concatenate([left, right], axis=1))
    first, last, home = lax.optimization_barrier((first, last, home))
    first = home_rows(first)
    return call(
        combine_kernel, shape((ROWS, model), BF16), routes, route_weight, first, last, home
    )


def solution(mesh):
    fine = Mesh(mesh.devices.reshape(4, 4, 4, 2), ("z", "y", "x", "core"))
    both = ("z", "y", "x", "core")
    return jax.shard_map(
        per_device,
        mesh=fine,
        in_specs=(
            P(SEQ, EXP),
            P(SEQ, EXP),
            P(SEQ, EXP),
            P(SEQ, EXP),
            P(SEQ, EXP),
            P(EXP),
            P(),
            P(both, None),
            P(both, None),
            P(EXP, None, SEQ),
            P(EXP, SEQ, None),
        ),
        out_specs=P(both, None),
        check_vma=False,
    )
```

```python
import jax
import jax.numpy as jnp
from jax import lax
from jax.experimental import pallas as pl
from jax.experimental.pallas import tpu as pltpu
from jax.sharding import Mesh
from jax.sharding import PartitionSpec as P

HEAD_DIM = 128
BLK = 256
EXPERTS = 8
CAP = 10
FIRST = 8
LAST = CAP - FIRST
SIDE = 4
TILE = 256
ROWS = 32
LOG_ROWS = 16
VMEM = 56 * 1024 * 1024
F32 = jnp.float32
BF16 = jnp.bfloat16
HIGH = lax.Precision.HIGHEST
SEQ = ("z", "y")
EXP = ("x", "core")


def params():
    return pltpu.CompilerParams(vmem_limit_bytes=VMEM)


def whole():
    return pl.BlockSpec(memory_space=pltpu.VMEM)


def call(kernel, out, *args):
    many = isinstance(out, (list, tuple))
    return pl.pallas_call(
        kernel,
        out_shape=out,
        in_specs=[whole()] * len(args),
        out_specs=[whole()] * len(out) if many else whole(),
        compiler_params=params(),
    )(*args)


def shape(dims, dtype):
    return jax.ShapeDtypeStruct(dims, dtype)


def split3(value):
    first = value.astype(BF16)
    rest = value - first.astype(F32)
    second = rest.astype(BF16)
    third = (rest - second.astype(F32)).astype(BF16)
    return first, second, third


def cumulated(decay):
    row = lax.broadcasted_iota(jnp.int32, (BLK, BLK), 0)
    col = lax.broadcasted_iota(jnp.int32, (BLK, BLK), 1)
    lower = (col <= row).astype(F32)
    return lax.dot_general(
        lower, decay, (((1,), (1,)), ((), ())), preferred_element_type=F32, precision=HIGH
    )


def log_lines(logs):
    heads = logs.shape[1]
    wide = jnp.concatenate([logs, jnp.zeros((1, HEAD_DIM - heads), F32)], axis=1)
    parts = [p.astype(F32) for p in split3(wide)]
    lines = jnp.concatenate(parts + [jnp.zeros((LOG_ROWS - 3, HEAD_DIM), F32)], axis=0)
    return lines.astype(BF16)


def state_kernel(key_ref, value_ref, decay_ref, out_ref):
    heads = decay_ref.shape[0]
    cumul = cumulated(decay_ref[...])
    total = cumul[BLK - 1 :, :]
    fading = jnp.exp(total - cumul)
    for h in range(heads):
        cols = slice(h * HEAD_DIM, (h + 1) * HEAD_DIM)
        faded = (fading[:, h : h + 1] * key_ref[:, cols].astype(F32)).astype(BF16)
        own = lax.dot_general(
            faded, value_ref[:, cols], (((0,), (0,)), ((), ())), preferred_element_type=F32
        )
        out_ref[cols, :] = own.astype(BF16)
    out_ref[heads * HEAD_DIM :, :] = log_lines(total)


def inner_kernel(query_ref, key_ref, value_ref, decay_ref, out_ref):
    heads = decay_ref.shape[0]
    decay = decay_ref[...]
    cumul = cumulated(decay)
    row = lax.broadcasted_iota(jnp.int32, (BLK, BLK), 0)
    col = lax.broadcasted_iota(jnp.int32, (BLK, BLK), 1)
    upper = (row <= col).astype(F32)
    across = jnp.dot(decay, upper, preferred_element_type=F32, precision=HIGH)
    causal = col <= row
    for h in range(heads):
        cols = slice(h * HEAD_DIM, (h + 1) * HEAD_DIM)
        scores = lax.dot_general(
            query_ref[:, cols],
            key_ref[:, cols],
            (((1,), (1,)), ((), ())),
            preferred_element_type=F32,
        )
        spread = cumul[:, h : h + 1] - across[h : h + 1, :]
        weights = jnp.where(causal, jnp.exp(jnp.where(causal, spread, 0.0)) * scores, 0.0)
        out_ref[:, cols] = jnp.dot(
            weights.astype(BF16), value_ref[:, cols], preferred_element_type=F32
        )


def read_logs(ref, heads):
    rows = ref[heads * HEAD_DIM :, :].astype(F32)
    return rows[0:1] + rows[1:2] + rows[2:3]


def line_kernel(place_ref, *refs):
    states, (line_ref, before_ref, log_ref) = refs[:SIDE], refs[SIDE:]
    heads = line_ref.shape[0] // HEAD_DIM
    mine = place_ref[1]
    spots = [lax.rem(mine - d + SIDE, SIDE) for d in range(SIDE)]
    logs = [read_logs(ref, heads) for ref in states]
    to_end, to_me = [], []
    for i in range(SIDE):
        later = [jnp.where(spots[j] > spots[i], logs[j], 0.0) for j in range(SIDE)]
        between = [jnp.where(spots[j] < mine, later[j], 0.0) for j in range(SIDE)]
        to_end.append(jnp.exp(sum(later)))
        to_me.append(jnp.where(spots[i] < mine, jnp.exp(sum(between)), 0.0))
    for h in range(heads):
        rows = slice(h * HEAD_DIM, (h + 1) * HEAD_DIM)
        end = jnp.zeros((HEAD_DIM, HEAD_DIM), F32)
        me = jnp.zeros((HEAD_DIM, HEAD_DIM), F32)
        for i in range(SIDE):
            state = states[i][rows, :].astype(F32)
            end = end + to_end[i][:, h : h + 1] * state
            me = me + to_me[i][:, h : h + 1] * state
        line_ref[rows, :] = end.astype(BF16)
        before_ref[rows, :] = me
    line_ref[heads * HEAD_DIM :, :] = log_lines(sum(logs)[:, :heads])
    before = [jnp.where(spots[i] < mine, logs[i], 0.0) for i in range(SIDE)]
    log_ref[...] = jnp.broadcast_to(sum(before), log_ref.shape)


def mix_kernel(
    query_ref,
    decay_ref,
    inner_ref,
    residual_ref,
    gain_ref,
    line1_ref,
    line2_ref,
    line3_ref,
    before_ref,
    log_ref,
    routes_ref,
    mixed_ref,
    packed_ref,
):
    heads = decay_ref.shape[0]
    lines = (line1_ref, line2_ref, line3_ref)
    logs = [read_logs(ref, heads) for ref in lines]
    here = log_ref[0:1, :]
    factors = [jnp.exp(sum(logs[:i], here)) for i in range(len(lines))]
    fade = jnp.exp(cumulated(decay_ref[...]))
    for h in range(heads):
        cols = slice(h * HEAD_DIM, (h + 1) * HEAD_DIM)
        state = before_ref[cols, :]
        for factor, ref in zip(factors, lines):
            state = state + factor[:, h : h + 1] * ref[cols, :].astype(F32)
        faded = fade[:, h : h + 1] * query_ref[:, cols].astype(F32)
        attention = inner_ref[:, cols] + jnp.dot(
            faded, state, preferred_element_type=F32, precision=HIGH
        )
        square = jnp.mean(attention * attention, axis=-1, keepdims=True)
        normed = attention * lax.rsqrt(square + 1e-06) * gain_ref[:, cols]
        mixed_ref[:, cols] = (residual_ref[:, cols].astype(F32) + normed).astype(BF16)
    token = lax.broadcasted_iota(jnp.int32, (EXPERTS, BLK), 1)
    expert = lax.broadcasted_iota(jnp.int32, (EXPERTS, BLK), 0)
    names = (expert == routes_ref[0:1, :]) | (expert == routes_ref[1:2, :])
    row = lax.broadcasted_iota(jnp.int32, (BLK, BLK), 0)
    col = lax.broadcasted_iota(jnp.int32, (BLK, BLK), 1)
    earlier = ((row < col) & (row // ROWS == col // ROWS)).astype(BF16)
    rank = jnp.dot(names.astype(BF16), earlier, preferred_element_type=F32).astype(jnp.int32)
    mixed = mixed_ref[...]
    block = token // ROWS
    early = rank < FIRST
    low = block * FIRST + rank
    high = BLK // ROWS * FIRST + block * LAST + rank - FIRST
    slot = jnp.where(names, jnp.where(early, low, high), -1)
    which = lax.broadcasted_iota(jnp.int32, (packed_ref.shape[1], BLK), 0)
    for e in range(EXPERTS):
        placer = (which == slot[e : e + 1, :]).astype(BF16)
        packed_ref[e] = jnp.dot(placer, mixed, preferred_element_type=F32).astype(BF16)


def norm_kernel(parts_ref, gain_ref, first_ref, left_ref, right_ref):
    parts, _, width = parts_ref.shape
    early, half = first_ref.shape[0], parts // 2
    square = 0.0
    for j in range(parts):
        value = parts_ref[j].astype(F32)
        square = square + jnp.sum(value * value, axis=-1, keepdims=True)
    scale = lax.rsqrt(square / (parts * width) + 1e-06)
    for j in range(parts):
        cols = slice(j * width, (j + 1) * width)
        value = (parts_ref[j].astype(F32) * scale * gain_ref[:, cols]).astype(BF16)
        first_ref[:, cols] = value[:early]
        side = left_ref if j < half else right_ref
        side[:, j % half * width : (j % half + 1) * width] = value[early:]


def expert_kernel(plan, counts, refs):
    inputs, outputs, parts = counts
    ins, up, down = refs[:inputs], refs[inputs], refs[inputs + 1]
    outs = refs[inputs + 2 : inputs + 2 + outputs]
    up_here, down_here, rows_here, out_here, weight_sem, in_sem, out_sem = refs[-7:]
    tiles, wide = len(plan), up.shape[1] // parts

    def weight_up(k):
        part = pl.ds(k * wide, wide)
        return pltpu.make_async_copy(up.at[0, part], up_here.at[part], weight_sem.at[k])

    def weight_down(k):
        part = pl.ds(k * wide, wide)
        return pltpu.make_async_copy(
            down.at[0, :, part], down_here.at[:, part], weight_sem.at[parts + k]
        )

    def pieces(t, arrays, here, sems, out):
        for i, (array, index, start, count, row, col) in enumerate(plan[t]):
            far = arrays[array].at[index, pl.ds(start, count)]
            near = here.at[t % 2, pl.ds(row, count), pl.ds(col, far.shape[1])]
            pair = (near, far) if out else (far, near)
            yield pltpu.make_async_copy(*pair, sems.at[t % 2, i])

    def read(t):
        return pieces(t, ins, rows_here, in_sem, False)

    def write(t):
        return pieces(t, outs, out_here, out_sem, True)

    for copy in read(0):
        copy.start()
    for k in range(parts):
        weight_up(k).start()

    def at(t, now, action):
        @pl.when(t == now)
        def _():
            action()

    def wait(copies):
        for copy in copies:
            copy.wait()

    def begin(copies):
        for copy in copies:
            copy.start()

    def step(t, carry):
        slot = lax.rem(t, 2)
        for now in range(tiles):
            at(t, now, lambda now=now: wait(read(now)))
        value = 0.0
        for k in range(parts):
            cols = pl.ds(k * wide, wide)
            at(t, 0, lambda k=k: weight_up(k).wait())
            at(t, 0, lambda k=k: weight_down(k).start())
            value = value + jnp.dot(
                rows_here[slot, :, cols], up_here[cols, :], preferred_element_type=F32
            )
        if tiles > 1:
            at(t, 0, lambda: begin(read(1)))
        hidden = (value / (1.0 + jnp.exp(-value))).astype(BF16)
        for now in range(2, tiles):
            at(t, now, lambda now=now: wait(write(now - 2)))
        for k in range(parts):
            cols = pl.ds(k * wide, wide)
            at(t, 0, lambda k=k: weight_down(k).wait())
            out_here[slot, :, cols] = jnp.dot(
                hidden, down_here[:, cols], preferred_element_type=F32
            ).astype(BF16)
        for now in range(tiles):
            at(t, now, lambda now=now: begin(write(now)))
        for now in range(tiles - 2):
            at(t, now, lambda now=now: begin(read(now + 2)))
        return carry

    lax.fori_loop(0, tiles, step, 0)
    for t in range(max(0, tiles - 2), tiles):
        wait(write(t))


def expert_call(plan, arrays, up_weight, down_weight, tile):
    units, width = down_weight.shape[1:]
    total = len(plan) * tile
    parts = 4
    most = max(len(p) for p in plan)
    counts = (len(arrays), len(arrays), parts)
    anywhere = pl.BlockSpec(memory_space=pl.ANY)

    def kernel(*refs):
        expert_kernel(plan, counts, refs)

    return pl.pallas_call(
        kernel,
        out_shape=[shape(a.shape, BF16) for a in arrays],
        in_specs=[anywhere] * (len(arrays) + 2),
        out_specs=[anywhere] * len(arrays),
        scratch_shapes=[
            pltpu.VMEM((width, units), BF16),
            pltpu.VMEM((units, width), BF16),
            pltpu.VMEM((2, tile, width), BF16),
            pltpu.VMEM((2, tile, width), BF16),
            pltpu.SemaphoreType.DMA((2 * parts,)),
            pltpu.SemaphoreType.DMA((2, most)),
            pltpu.SemaphoreType.DMA((2, most)),
        ],
        compiler_params=params(),
        cost_estimate=pl.CostEstimate(
            flops=6 * total * width * units,
            bytes_accessed=4 * (total + units) * width,
            transcendentals=total * units,
        ),
    )(*arrays, up_weight, down_weight)


def rows_kernel(rows_ref, up_ref, down_ref, out_ref):
    value = jnp.dot(rows_ref[...], up_ref[...], preferred_element_type=F32)
    hidden = (value / (1.0 + jnp.exp(-value))).astype(BF16)
    out_ref[...] = jnp.dot(hidden, down_ref[...], preferred_element_type=F32).astype(BF16)


def expert_rows(rows, up_weight, down_weight):
    total, width = rows.shape
    units = up_weight.shape[-1]
    once = pl.Buffered(1)
    return pl.pallas_call(
        rows_kernel,
        grid=(total // TILE,),
        out_shape=shape((total, width), BF16),
        in_specs=[
            pl.BlockSpec((TILE, width), lambda i: (i, 0)),
            pl.BlockSpec((None, width, units), lambda i: (0, 0, 0), pipeline_mode=once),
            pl.BlockSpec((None, units, width), lambda i: (0, 0, 0), pipeline_mode=once),
        ],
        out_specs=pl.BlockSpec((TILE, width), lambda i: (i, 0)),
        compiler_params=params(),
        cost_estimate=pl.CostEstimate(
            flops=4 * total * width * units,
            bytes_accessed=4 * (total + units) * width,
            transcendentals=total * units,
        ),
    )(rows, up_weight, down_weight)


def expert_halves(left, right, up_weight, down_weight):
    arrays = [a for pair in left + right for a in pair]
    _, rows, half = left[0][0].shape
    plan = [[] for _ in range(SIDE * SIDE * rows // TILE)]
    for z in range(SIDE):
        for y in range(SIDE):
            done = 0
            while done < rows:
                t, row = divmod((z * SIDE + y) * rows + done, TILE)
                count = min(rows - done, TILE - row)
                plan[t].append((2 * z + y // 2, y % 2, done, count, row, 0))
                plan[t].append((2 * (SIDE + y) + z // 2, z % 2, done, count, row, half))
                done += count
    out = expert_call(plan, arrays, up_weight, down_weight, TILE)
    pairs = [(out[2 * i], out[2 * i + 1]) for i in range(2 * SIDE)]
    return pairs[:SIDE], pairs[SIDE:]


def shift(value, axis, step, count=SIDE):
    return lax.ppermute(value, axis, [(i, (i + step) % count) for i in range(count)])


def gather_near(value, axis):
    ring = [value] + [shift(value, axis, d) for d in range(1, SIDE)]
    return jnp.stack(ring[:2]), jnp.stack(ring[2:])


def gather_start(low, high, axis):
    low_after, high_before = shift(low, axis, 1), shift(high, axis, -1)
    return low_after, high_before, shift(high, axis, 1), shift(low, axis, -1)


def gather_end(low, high, started, axis):
    low_after, high_before, high_after, low_before = started
    far = (shift(low_after, axis, 1), shift(high_before, axis, -1))
    return [(low, high), (low_after, high_after), far, (low_before, high_before)]


def total_of(*terms):
    return sum(t.astype(F32) for t in terms).astype(BF16)


def scatter_near(low, high, axis):
    return total_of(
        low[0], shift(low[1], axis, -1), shift(high[0], axis, 2), shift(high[1], axis, 1)
    )


def scatter_start(value, axis):
    to_after = shift(value[2][0], axis, 1)
    to_before = shift(value[2][1], axis, -1)
    return to_after, to_before, shift(value[3][1], axis, 1), shift(value[1][0], axis, -1)


def scatter_end(value, started, axis):
    to_after, to_before, high_after, low_before = started
    low_after = shift(total_of(value[3][0], to_after), axis, 1)
    high_before = shift(total_of(value[1][1], to_before), axis, -1)
    return total_of(value[0][0], low_after, low_before), total_of(
        value[0][1], high_after, high_before
    )


def home_rows(summed):
    lines = summed.reshape(EXPERTS, -1, HEAD_DIM)
    back = lax.all_to_all(lines, EXP, split_axis=0, concat_axis=0, tiled=True)
    return back.reshape(summed.shape)


def chip_routes(routes):
    ours = lax.axis_index("core")
    other = shift(routes, "core", 1, 2)
    return jnp.where(ours == 0, jnp.stack([routes, other]), jnp.stack([other, routes]))


def gather_routes(pair):
    ring = jnp.stack([pair] + [shift(pair, "x", d) for d in range(1, SIDE)])
    distance = (lax.axis_index("x") - jnp.arange(SIDE)) % SIDE
    placed = sum(
        jnp.where((distance == d)[:, None, None, None], ring[d][None], 0) for d in range(SIDE)
    )
    return jnp.transpose(placed, (2, 0, 1, 3)).reshape(2, -1)


def combine_kernel(routes_ref, weight_ref, first_ref, last_ref, mixed_ref, out_ref):
    rows = out_ref.shape[0]
    routes = routes_ref[...]
    expert = lax.broadcasted_iota(jnp.int32, (rows, EXPERTS), 1)
    names = [expert == routes[:, i : i + 1] for i in range(2)]
    row = lax.broadcasted_iota(jnp.int32, (rows, rows), 0)
    col = lax.broadcasted_iota(jnp.int32, (rows, rows), 1)
    earlier = (col < row).astype(BF16)
    ranks = jnp.dot(
        earlier, (names[0] | names[1]).astype(BF16), preferred_element_type=F32
    ).astype(jnp.int32)
    chunks = []
    for ref, low, size in ((first_ref, 0, FIRST), (last_ref, FIRST, LAST)):
        place = lax.broadcasted_iota(jnp.int32, (rows, EXPERTS * size), 1)
        blend = jnp.zeros((rows, EXPERTS * size), F32)
        for i in range(2):
            rank = jnp.sum(jnp.where(names[i], ranks, 0), axis=1, keepdims=True)
            slot = routes[:, i : i + 1] * size + rank - low
            taken = (place == slot) & (rank >= low) & (rank < low + size)
            blend = blend + jnp.where(taken, weight_ref[:, i : i + 1], 0.0)
        chunks.append((ref, split3(blend)))
    width = mixed_ref.shape[2]
    for j in range(mixed_ref.shape[0]):
        cols = slice(j * width, (j + 1) * width)
        value = mixed_ref[j].astype(F32)
        for ref, parts in chunks:
            for p in parts:
                value = value + jnp.dot(p, ref[:, cols], preferred_element_type=F32)
        out_ref[:, cols] = value.astype(BF16)


def per_device(
    queries,
    key_rows,
    value_rows,
    log_decay,
    residual,
    head_gain,
    moe_gain,
    routes,
    route_weight,
    up_weight,
    down_weight,
):
    token_count, width = queries.shape
    heads = log_decay.shape[1]
    half = moe_gain.shape[0] // 2
    model = moe_gain.shape[0]
    exp_count = model // width
    blocks = token_count // ROWS
    place = jnp.stack([lax.axis_index("z"), lax.axis_index("y")]).astype(jnp.int32)
    chip = chip_routes(routes.T)
    log_decay = log_decay.T

    state_rows = heads * HEAD_DIM + LOG_ROWS
    sent = call(state_kernel, shape((state_rows, HEAD_DIM), BF16), key_rows, value_rows, log_decay)
    in_line = [sent] + [shift(sent, "y", d) for d in range(1, SIDE)]
    inner = call(
        inner_kernel, shape((token_count, width), F32), queries, key_rows, value_rows, log_decay
    )
    in_line, inner, chip = lax.optimization_barrier((in_line, inner, chip))
    all_routes = gather_routes(chip)
    scalar = pl.BlockSpec(memory_space=pltpu.SMEM)
    line, before, line_log = pl.pallas_call(
        line_kernel,
        out_shape=[
            shape((state_rows, HEAD_DIM), BF16),
            shape((heads * HEAD_DIM, HEAD_DIM), F32),
            shape((8, HEAD_DIM), F32),
        ],
        in_specs=[scalar] + [whole()] * SIDE,
        out_specs=[whole()] * 3,
        compiler_params=params(),
    )(place, *in_line)
    lines = [
        lax.ppermute(line, "z", [(i, i + d) for i in range(SIDE - d)]) for d in range(1, SIDE)
    ]
    mixed, packed = pl.pallas_call(
        mix_kernel,
        out_shape=[
            shape((token_count, width), BF16),
            shape((EXPERTS, blocks * CAP, width), BF16),
        ],
        in_specs=[whole()] * 11,
        out_specs=[whole()] * 2,
        compiler_params=params(),
    )(
        queries,
        log_decay,
        inner,
        residual,
        head_gain.reshape(1, width),
        *lines,
        before,
        line_log,
        all_routes,
    )
    parts = lax.all_to_all(packed, EXP, split_axis=0, concat_axis=0, tiled=True)
    normed, left, right = call(
        norm_kernel,
        [shape((blocks * FIRST, model), BF16)] + [shape((blocks * LAST, half), BF16)] * 2,
        parts,
        moe_gain.reshape(1, model),
    )
    rows = lax.all_gather(normed, SEQ, axis=0, tiled=True)
    left, right = gather_near(left, "y"), gather_near(right, "z")
    left = gather_end(*left, gather_start(*left, "z"), "z")
    right = gather_end(*right, gather_start(*right, "y"), "y")
    left, right = expert_halves(left, right, up_weight, down_weight)
    starts = scatter_start(left, "z"), scatter_start(right, "y")
    rows, starts = lax.optimization_barrier((rows, starts))
    left = scatter_end(left, starts[0], "z")
    right = scatter_end(right, starts[1], "y")

    partial = expert_rows(rows, up_weight, down_weight)
    first = lax.psum_scatter(partial, SEQ, scatter_dimension=0, tiled=True)
    mixed, _ = lax.optimization_barrier((mixed, partial))
    home = lax.all_to_all(
        mixed.reshape(exp_count, ROWS, width), EXP, split_axis=0, concat_axis=0, tiled=True
    )
    left, right = scatter_near(*left, "y"), scatter_near(*right, "z")
    last = home_rows(jnp.concatenate([left, right], axis=1))
    first, last, home = lax.optimization_barrier((first, last, home))
    first = home_rows(first)
    return call(
        combine_kernel, shape((ROWS, model), BF16), routes, route_weight, first, last, home
    )


def solution(mesh):
    fine = Mesh(mesh.devices.reshape(4, 4, 4, 2), ("z", "y", "x", "core"))
    both = ("z", "y", "x", "core")
    return jax.shard_map(
        per_device,
        mesh=fine,
        in_specs=(
            P(SEQ, EXP),
            P(SEQ, EXP),
            P(SEQ, EXP),
            P(SEQ, EXP),
            P(SEQ, EXP),
            P(EXP),
            P(),
            P(both, None),
            P(both, None),
            P(EXP, None, SEQ),
            P(EXP, SEQ, None),
        ),
        out_specs=P(both, None),
        check_vma=False,
    )
```

```python
import jax
import jax.numpy as jnp
from jax import lax
from jax.experimental import pallas as pl
from jax.experimental.pallas import tpu as pltpu
from jax.sharding import Mesh
from jax.sharding import PartitionSpec as P

HEAD_DIM = 128
BLK = 256
EXPERTS = 8
CAP = 10
FIRST = 8
LAST = CAP - FIRST
SIDE = 4
TILE = 256
ROWS = 32
LOG_ROWS = 16
VMEM = 56 * 1024 * 1024
F32 = jnp.float32
BF16 = jnp.bfloat16
HIGH = lax.Precision.HIGHEST
SEQ = ("z", "y")
EXP = ("x", "core")


def params():
    return pltpu.CompilerParams(vmem_limit_bytes=VMEM)


def whole():
    return pl.BlockSpec(memory_space=pltpu.VMEM)


def call(kernel, out, *args):
    many = isinstance(out, (list, tuple))
    return pl.pallas_call(
        kernel,
        out_shape=out,
        in_specs=[whole()] * len(args),
        out_specs=[whole()] * len(out) if many else whole(),
        compiler_params=params(),
    )(*args)


def shape(dims, dtype):
    return jax.ShapeDtypeStruct(dims, dtype)


def split3(value):
    first = value.astype(BF16)
    rest = value - first.astype(F32)
    second = rest.astype(BF16)
    third = (rest - second.astype(F32)).astype(BF16)
    return first, second, third


def cumulated(decay):
    row = lax.broadcasted_iota(jnp.int32, (BLK, BLK), 0)
    col = lax.broadcasted_iota(jnp.int32, (BLK, BLK), 1)
    lower = (col <= row).astype(F32)
    return lax.dot_general(
        lower, decay, (((1,), (1,)), ((), ())), preferred_element_type=F32, precision=HIGH
    )


def log_lines(logs):
    heads = logs.shape[1]
    wide = jnp.concatenate([logs, jnp.zeros((1, HEAD_DIM - heads), F32)], axis=1)
    parts = [p.astype(F32) for p in split3(wide)]
    lines = jnp.concatenate(parts + [jnp.zeros((LOG_ROWS - 3, HEAD_DIM), F32)], axis=0)
    return lines.astype(BF16)


def state_kernel(key_ref, value_ref, decay_ref, out_ref):
    heads = decay_ref.shape[0]
    cumul = cumulated(decay_ref[...])
    total = cumul[BLK - 1 :, :]
    fading = jnp.exp(total - cumul)
    for h in range(heads):
        cols = slice(h * HEAD_DIM, (h + 1) * HEAD_DIM)
        faded = (fading[:, h : h + 1] * key_ref[:, cols].astype(F32)).astype(BF16)
        own = lax.dot_general(
            faded, value_ref[:, cols], (((0,), (0,)), ((), ())), preferred_element_type=F32
        )
        out_ref[cols, :] = own.astype(BF16)
    out_ref[heads * HEAD_DIM :, :] = log_lines(total)


def inner_kernel(query_ref, key_ref, value_ref, decay_ref, out_ref):
    heads = decay_ref.shape[0]
    decay = decay_ref[...]
    cumul = cumulated(decay)
    row = lax.broadcasted_iota(jnp.int32, (BLK, BLK), 0)
    col = lax.broadcasted_iota(jnp.int32, (BLK, BLK), 1)
    upper = (row <= col).astype(F32)
    across = jnp.dot(decay, upper, preferred_element_type=F32, precision=HIGH)
    causal = col <= row
    for h in range(heads):
        cols = slice(h * HEAD_DIM, (h + 1) * HEAD_DIM)
        scores = lax.dot_general(
            query_ref[:, cols],
            key_ref[:, cols],
            (((1,), (1,)), ((), ())),
            preferred_element_type=F32,
        )
        spread = cumul[:, h : h + 1] - across[h : h + 1, :]
        weights = jnp.where(causal, jnp.exp(jnp.where(causal, spread, 0.0)) * scores, 0.0)
        out_ref[:, cols] = jnp.dot(
            weights.astype(BF16), value_ref[:, cols], preferred_element_type=F32
        )


def read_logs(ref, heads):
    rows = ref[heads * HEAD_DIM :, :].astype(F32)
    return rows[0:1] + rows[1:2] + rows[2:3]


def line_kernel(place_ref, *refs):
    states, (line_ref, before_ref, log_ref) = refs[:SIDE], refs[SIDE:]
    heads = line_ref.shape[0] // HEAD_DIM
    mine = place_ref[1]
    spots = [lax.rem(mine - d + SIDE, SIDE) for d in range(SIDE)]
    logs = [read_logs(ref, heads) for ref in states]
    to_end, to_me = [], []
    for i in range(SIDE):
        later = [jnp.where(spots[j] > spots[i], logs[j], 0.0) for j in range(SIDE)]
        between = [jnp.where(spots[j] < mine, later[j], 0.0) for j in range(SIDE)]
        to_end.append(jnp.exp(sum(later)))
        to_me.append(jnp.where(spots[i] < mine, jnp.exp(sum(between)), 0.0))
    for h in range(heads):
        rows = slice(h * HEAD_DIM, (h + 1) * HEAD_DIM)
        end = jnp.zeros((HEAD_DIM, HEAD_DIM), F32)
        me = jnp.zeros((HEAD_DIM, HEAD_DIM), F32)
        for i in range(SIDE):
            state = states[i][rows, :].astype(F32)
            end = end + to_end[i][:, h : h + 1] * state
            me = me + to_me[i][:, h : h + 1] * state
        line_ref[rows, :] = end.astype(BF16)
        before_ref[rows, :] = me
    line_ref[heads * HEAD_DIM :, :] = log_lines(sum(logs)[:, :heads])
    before = [jnp.where(spots[i] < mine, logs[i], 0.0) for i in range(SIDE)]
    log_ref[...] = jnp.broadcast_to(sum(before), log_ref.shape)


def mix_kernel(
    query_ref,
    decay_ref,
    inner_ref,
    residual_ref,
    gain_ref,
    line1_ref,
    line2_ref,
    line3_ref,
    before_ref,
    log_ref,
    routes_ref,
    mixed_ref,
    packed_ref,
):
    heads = decay_ref.shape[0]
    lines = (line1_ref, line2_ref, line3_ref)
    logs = [read_logs(ref, heads) for ref in lines]
    here = log_ref[0:1, :]
    factors = [jnp.exp(sum(logs[:i], here)) for i in range(len(lines))]
    fade = jnp.exp(cumulated(decay_ref[...]))
    for h in range(heads):
        cols = slice(h * HEAD_DIM, (h + 1) * HEAD_DIM)
        state = before_ref[cols, :]
        for factor, ref in zip(factors, lines):
            state = state + factor[:, h : h + 1] * ref[cols, :].astype(F32)
        faded = fade[:, h : h + 1] * query_ref[:, cols].astype(F32)
        attention = inner_ref[:, cols] + jnp.dot(
            faded, state, preferred_element_type=F32, precision=HIGH
        )
        square = jnp.mean(attention * attention, axis=-1, keepdims=True)
        normed = attention * lax.rsqrt(square + 1e-06) * gain_ref[:, cols]
        mixed_ref[:, cols] = (residual_ref[:, cols].astype(F32) + normed).astype(BF16)
    token = lax.broadcasted_iota(jnp.int32, (EXPERTS, BLK), 1)
    expert = lax.broadcasted_iota(jnp.int32, (EXPERTS, BLK), 0)
    names = (expert == routes_ref[0:1, :]) | (expert == routes_ref[1:2, :])
    row = lax.broadcasted_iota(jnp.int32, (BLK, BLK), 0)
    col = lax.broadcasted_iota(jnp.int32, (BLK, BLK), 1)
    earlier = ((row < col) & (row // ROWS == col // ROWS)).astype(BF16)
    rank = jnp.dot(names.astype(BF16), earlier, preferred_element_type=F32).astype(jnp.int32)
    mixed = mixed_ref[...]
    block = token // ROWS
    early = rank < FIRST
    low = block * FIRST + rank
    high = BLK // ROWS * FIRST + block * LAST + rank - FIRST
    slot = jnp.where(names, jnp.where(early, low, high), -1)
    which = lax.broadcasted_iota(jnp.int32, (packed_ref.shape[1], BLK), 0)
    for e in range(EXPERTS):
        placer = (which == slot[e : e + 1, :]).astype(BF16)
        packed_ref[e] = jnp.dot(placer, mixed, preferred_element_type=F32).astype(BF16)


def norm_kernel(parts_ref, gain_ref, first_ref, left_ref, right_ref):
    parts, _, width = parts_ref.shape
    early, half = first_ref.shape[0], parts // 2
    square = 0.0
    for j in range(parts):
        value = parts_ref[j].astype(F32)
        square = square + jnp.sum(value * value, axis=-1, keepdims=True)
    scale = lax.rsqrt(square / (parts * width) + 1e-06)
    for j in range(parts):
        cols = slice(j * width, (j + 1) * width)
        value = (parts_ref[j].astype(F32) * scale * gain_ref[:, cols]).astype(BF16)
        first_ref[:, cols] = value[:early]
        side = left_ref if j < half else right_ref
        side[:, j % half * width : (j % half + 1) * width] = value[early:]


def expert_kernel(plan, counts, refs):
    inputs, outputs, parts = counts
    ins, up, down = refs[:inputs], refs[inputs], refs[inputs + 1]
    outs = refs[inputs + 2 : inputs + 2 + outputs]
    up_here, down_here, rows_here, out_here, weight_sem, in_sem, out_sem = refs[-7:]
    tiles, wide = len(plan), up.shape[1] // parts

    def weight_up(k):
        part = pl.ds(k * wide, wide)
        return pltpu.make_async_copy(up.at[0, part], up_here.at[part], weight_sem.at[k])

    def weight_down(k):
        part = pl.ds(k * wide, wide)
        return pltpu.make_async_copy(
            down.at[0, :, part], down_here.at[:, part], weight_sem.at[parts + k]
        )

    def pieces(t, arrays, here, sems, out):
        for i, (array, index, start, count, row, col) in enumerate(plan[t]):
            far = arrays[array].at[index, pl.ds(start, count)]
            near = here.at[t % 2, pl.ds(row, count), pl.ds(col, far.shape[1])]
            pair = (near, far) if out else (far, near)
            yield pltpu.make_async_copy(*pair, sems.at[t % 2, i])

    def read(t):
        return pieces(t, ins, rows_here, in_sem, False)

    def write(t):
        return pieces(t, outs, out_here, out_sem, True)

    for copy in read(0):
        copy.start()
    for k in range(parts):
        weight_up(k).start()

    def at(t, now, action):
        @pl.when(t == now)
        def _():
            action()

    def wait(copies):
        for copy in copies:
            copy.wait()

    def begin(copies):
        for copy in copies:
            copy.start()

    def step(t, carry):
        slot = lax.rem(t, 2)
        for now in range(tiles):
            at(t, now, lambda now=now: wait(read(now)))
        value = 0.0
        for k in range(parts):
            cols = pl.ds(k * wide, wide)
            at(t, 0, lambda k=k: weight_up(k).wait())
            at(t, 0, lambda k=k: weight_down(k).start())
            value = value + jnp.dot(
                rows_here[slot, :, cols], up_here[cols, :], preferred_element_type=F32
            )
        if tiles > 1:
            at(t, 0, lambda: begin(read(1)))
        hidden = (value / (1.0 + jnp.exp(-value))).astype(BF16)
        for now in range(2, tiles):
            at(t, now, lambda now=now: wait(write(now - 2)))
        for k in range(parts):
            cols = pl.ds(k * wide, wide)
            at(t, 0, lambda k=k: weight_down(k).wait())
            out_here[slot, :, cols] = jnp.dot(
                hidden, down_here[:, cols], preferred_element_type=F32
            ).astype(BF16)
        for now in range(tiles):
            at(t, now, lambda now=now: begin(write(now)))
        for now in range(tiles - 2):
            at(t, now, lambda now=now: begin(read(now + 2)))
        return carry

    lax.fori_loop(0, tiles, step, 0)
    for t in range(max(0, tiles - 2), tiles):
        wait(write(t))


def expert_call(plan, arrays, up_weight, down_weight, tile):
    units, width = down_weight.shape[1:]
    total = len(plan) * tile
    parts = 4
    most = max(len(p) for p in plan)
    counts = (len(arrays), len(arrays), parts)
    anywhere = pl.BlockSpec(memory_space=pl.ANY)

    def kernel(*refs):
        expert_kernel(plan, counts, refs)

    return pl.pallas_call(
        kernel,
        out_shape=[shape(a.shape, BF16) for a in arrays],
        in_specs=[anywhere] * (len(arrays) + 2),
        out_specs=[anywhere] * len(arrays),
        scratch_shapes=[
            pltpu.VMEM((width, units), BF16),
            pltpu.VMEM((units, width), BF16),
            pltpu.VMEM((2, tile, width), BF16),
            pltpu.VMEM((2, tile, width), BF16),
            pltpu.SemaphoreType.DMA((2 * parts,)),
            pltpu.SemaphoreType.DMA((2, most)),
            pltpu.SemaphoreType.DMA((2, most)),
        ],
        compiler_params=params(),
        cost_estimate=pl.CostEstimate(
            flops=6 * total * width * units,
            bytes_accessed=4 * (total + units) * width,
            transcendentals=total * units,
        ),
    )(*arrays, up_weight, down_weight)


def rows_kernel(rows_ref, up_ref, down_ref, out_ref):
    value = jnp.dot(rows_ref[...], up_ref[...], preferred_element_type=F32)
    hidden = (value / (1.0 + jnp.exp(-value))).astype(BF16)
    out_ref[...] = jnp.dot(hidden, down_ref[...], preferred_element_type=F32).astype(BF16)


def expert_rows(rows, up_weight, down_weight):
    total, width = rows.shape
    units = up_weight.shape[-1]
    once = pl.Buffered(1)
    return pl.pallas_call(
        rows_kernel,
        grid=(total // TILE,),
        out_shape=shape((total, width), BF16),
        in_specs=[
            pl.BlockSpec((TILE, width), lambda i: (i, 0)),
            pl.BlockSpec((None, width, units), lambda i: (0, 0, 0), pipeline_mode=once),
            pl.BlockSpec((None, units, width), lambda i: (0, 0, 0), pipeline_mode=once),
        ],
        out_specs=pl.BlockSpec((TILE, width), lambda i: (i, 0)),
        compiler_params=params(),
        cost_estimate=pl.CostEstimate(
            flops=4 * total * width * units,
            bytes_accessed=4 * (total + units) * width,
            transcendentals=total * units,
        ),
    )(rows, up_weight, down_weight)


def expert_halves(left, right, up_weight, down_weight):
    arrays = [a for pair in left + right for a in pair]
    _, rows, half = left[0][0].shape
    plan = [[] for _ in range(SIDE * SIDE * rows // TILE)]
    for z in range(SIDE):
        for y in range(SIDE):
            done = 0
            while done < rows:
                t, row = divmod((z * SIDE + y) * rows + done, TILE)
                count = min(rows - done, TILE - row)
                plan[t].append((2 * z + y // 2, y % 2, done, count, row, 0))
                plan[t].append((2 * (SIDE + y) + z // 2, z % 2, done, count, row, half))
                done += count
    out = expert_call(plan, arrays, up_weight, down_weight, TILE)
    pairs = [(out[2 * i], out[2 * i + 1]) for i in range(2 * SIDE)]
    return pairs[:SIDE], pairs[SIDE:]


def shift(value, axis, step, count=SIDE):
    return lax.ppermute(value, axis, [(i, (i + step) % count) for i in range(count)])


def gather_near(value, axis):
    ring = [value] + [shift(value, axis, d) for d in range(1, SIDE)]
    return jnp.stack(ring[:2]), jnp.stack(ring[2:])


def gather_start(low, high, axis):
    low_after, high_before = shift(low, axis, 1), shift(high, axis, -1)
    return low_after, high_before, shift(high, axis, 1), shift(low, axis, -1)


def gather_end(low, high, started, axis):
    low_after, high_before, high_after, low_before = started
    far = (shift(low_after, axis, 1), shift(high_before, axis, -1))
    return [(low, high), (low_after, high_after), far, (low_before, high_before)]


def total_of(*terms):
    return sum(t.astype(F32) for t in terms).astype(BF16)


def scatter_near(low, high, axis):
    return total_of(
        low[0], shift(low[1], axis, -1), shift(high[0], axis, 2), shift(high[1], axis, 1)
    )


def scatter_start(value, axis):
    to_after = shift(value[2][0], axis, 1)
    to_before = shift(value[2][1], axis, -1)
    return to_after, to_before, shift(value[3][1], axis, 1), shift(value[1][0], axis, -1)


def scatter_end(value, started, axis):
    to_after, to_before, high_after, low_before = started
    low_after = shift(total_of(value[3][0], to_after), axis, 1)
    high_before = shift(total_of(value[1][1], to_before), axis, -1)
    return total_of(value[0][0], low_after, low_before), total_of(
        value[0][1], high_after, high_before
    )


def home_rows(summed):
    rows, model = summed.shape
    each = rows // EXPERTS
    whole_tiles = each % 8 == 0
    lines = summed.reshape((EXPERTS, each, model) if whole_tiles else (EXPERTS, -1, HEAD_DIM))
    back = lax.all_to_all(lines, EXP, split_axis=0, concat_axis=0, tiled=True)
    return back.reshape(summed.shape)


def chip_routes(routes):
    ours = lax.axis_index("core")
    other = shift(routes, "core", 1, 2)
    return jnp.where(ours == 0, jnp.stack([routes, other]), jnp.stack([other, routes]))


def gather_routes(pair):
    ring = jnp.stack([pair] + [shift(pair, "x", d) for d in range(1, SIDE)])
    distance = (lax.axis_index("x") - jnp.arange(SIDE)) % SIDE
    placed = sum(
        jnp.where((distance == d)[:, None, None, None], ring[d][None], 0) for d in range(SIDE)
    )
    return jnp.transpose(placed, (2, 0, 1, 3)).reshape(2, -1)


def combine_kernel(routes_ref, weight_ref, first_ref, last_ref, mixed_ref, out_ref):
    rows = out_ref.shape[0]
    routes = routes_ref[...]
    expert = lax.broadcasted_iota(jnp.int32, (rows, EXPERTS), 1)
    names = [expert == routes[:, i : i + 1] for i in range(2)]
    row = lax.broadcasted_iota(jnp.int32, (rows, rows), 0)
    col = lax.broadcasted_iota(jnp.int32, (rows, rows), 1)
    earlier = (col < row).astype(BF16)
    ranks = jnp.dot(
        earlier, (names[0] | names[1]).astype(BF16), preferred_element_type=F32
    ).astype(jnp.int32)
    chunks = []
    for ref, low, size in ((first_ref, 0, FIRST), (last_ref, FIRST, LAST)):
        place = lax.broadcasted_iota(jnp.int32, (rows, EXPERTS * size), 1)
        blend = jnp.zeros((rows, EXPERTS * size), F32)
        for i in range(2):
            rank = jnp.sum(jnp.where(names[i], ranks, 0), axis=1, keepdims=True)
            slot = routes[:, i : i + 1] * size + rank - low
            taken = (place == slot) & (rank >= low) & (rank < low + size)
            blend = blend + jnp.where(taken, weight_ref[:, i : i + 1], 0.0)
        chunks.append((ref, split3(blend)))
    width = mixed_ref.shape[2]
    for j in range(mixed_ref.shape[0]):
        cols = slice(j * width, (j + 1) * width)
        value = mixed_ref[j].astype(F32)
        for ref, parts in chunks:
            for p in parts:
                value = value + jnp.dot(p, ref[:, cols], preferred_element_type=F32)
        out_ref[:, cols] = value.astype(BF16)


def per_device(
    queries,
    key_rows,
    value_rows,
    log_decay,
    residual,
    head_gain,
    moe_gain,
    routes,
    route_weight,
    up_weight,
    down_weight,
):
    token_count, width = queries.shape
    heads = log_decay.shape[1]
    half = moe_gain.shape[0] // 2
    model = moe_gain.shape[0]
    exp_count = model // width
    blocks = token_count // ROWS
    place = jnp.stack([lax.axis_index("z"), lax.axis_index("y")]).astype(jnp.int32)
    chip = chip_routes(routes.T)
    log_decay = log_decay.T

    state_rows = heads * HEAD_DIM + LOG_ROWS
    sent = call(state_kernel, shape((state_rows, HEAD_DIM), BF16), key_rows, value_rows, log_decay)
    in_line = [sent] + [shift(sent, "y", d) for d in range(1, SIDE)]
    inner = call(
        inner_kernel, shape((token_count, width), F32), queries, key_rows, value_rows, log_decay
    )
    in_line, inner, chip = lax.optimization_barrier((in_line, inner, chip))
    all_routes = gather_routes(chip)
    scalar = pl.BlockSpec(memory_space=pltpu.SMEM)
    line, before, line_log = pl.pallas_call(
        line_kernel,
        out_shape=[
            shape((state_rows, HEAD_DIM), BF16),
            shape((heads * HEAD_DIM, HEAD_DIM), F32),
            shape((8, HEAD_DIM), F32),
        ],
        in_specs=[scalar] + [whole()] * SIDE,
        out_specs=[whole()] * 3,
        compiler_params=params(),
    )(place, *in_line)
    lines = [
        lax.ppermute(line, "z", [(i, i + d) for i in range(SIDE - d)]) for d in range(1, SIDE)
    ]
    mixed, packed = pl.pallas_call(
        mix_kernel,
        out_shape=[
            shape((token_count, width), BF16),
            shape((EXPERTS, blocks * CAP, width), BF16),
        ],
        in_specs=[whole()] * 11,
        out_specs=[whole()] * 2,
        compiler_params=params(),
    )(
        queries,
        log_decay,
        inner,
        residual,
        head_gain.reshape(1, width),
        *lines,
        before,
        line_log,
        all_routes,
    )
    parts = lax.all_to_all(packed, EXP, split_axis=0, concat_axis=0, tiled=True)
    normed, left, right = call(
        norm_kernel,
        [shape((blocks * FIRST, model), BF16)] + [shape((blocks * LAST, half), BF16)] * 2,
        parts,
        moe_gain.reshape(1, model),
    )
    rows = lax.all_gather(normed, SEQ, axis=0, tiled=True)
    left, right = gather_near(left, "y"), gather_near(right, "z")
    left = gather_end(*left, gather_start(*left, "z"), "z")
    right = gather_end(*right, gather_start(*right, "y"), "y")
    left, right = expert_halves(left, right, up_weight, down_weight)
    starts = scatter_start(left, "z"), scatter_start(right, "y")
    rows, starts = lax.optimization_barrier((rows, starts))
    left = scatter_end(left, starts[0], "z")
    right = scatter_end(right, starts[1], "y")

    partial = expert_rows(rows, up_weight, down_weight)
    first = lax.psum_scatter(partial, SEQ, scatter_dimension=0, tiled=True)
    mixed, _ = lax.optimization_barrier((mixed, partial))
    home = lax.all_to_all(
        mixed.reshape(exp_count, ROWS, width), EXP, split_axis=0, concat_axis=0, tiled=True
    )
    left, right = scatter_near(*left, "y"), scatter_near(*right, "z")
    last = home_rows(jnp.concatenate([left, right], axis=1))
    first, last, home = lax.optimization_barrier((first, last, home))
    first = home_rows(first)
    return call(
        combine_kernel, shape((ROWS, model), BF16), routes, route_weight, first, last, home
    )


def solution(mesh):
    fine = Mesh(mesh.devices.reshape(4, 4, 4, 2), ("z", "y", "x", "core"))
    both = ("z", "y", "x", "core")
    return jax.shard_map(
        per_device,
        mesh=fine,
        in_specs=(
            P(SEQ, EXP),
            P(SEQ, EXP),
            P(SEQ, EXP),
            P(SEQ, EXP),
            P(SEQ, EXP),
            P(EXP),
            P(),
            P(both, None),
            P(both, None),
            P(EXP, None, SEQ),
            P(EXP, SEQ, None),
        ),
        out_specs=P(both, None),
        check_vma=False,
    )
```
